32 devices in a mesh: prow: 4 (over z), pcol: 8 (over y, x, core).
Axes of the slice: x: 2, y: 2, z: 4, core: 2. Of those that a mesh axis runs over, the one named last changes fastest.
Arguments:
- kernel: float32 [16, 4, 256, 8, 8, 256], P(None, 'prow', None, None, 'pcol'), may hold values from 0 to 1.5, as said below
- pivots: int32 [2], replicated, may hold values from 0 to 63, as said below
Outputs:
- panels: float32 [2, 16, 4, 256, 256], P(None, None, 'prow')
- trailing: float32 [16, 4, 256, 8, 8, 256], P(None, 'prow', None, None, 'pcol')
The draws below stay inside these ranges and needn't reach their ends.
Inputs may be any that keep to these rules, and one draw needn't show every extreme that they name: `kernel`: symmetric; a positive semidefinite matrix plus 0.5 times the identity. `pivots`: two different block numbers; one of them is the newest block, 63, in either position.
All inputs are finite; a program needn't handle non-finite values.
Results may differ from the reference program's by a relative error of at most 0.0003.
Values sent between devices are 32-bit elements; how exact they have to be, the bound alone decides.
A program may use at most 192 MiB of HBM per device.

```python
import jax
import jax.numpy as jnp
from jax import lax

M = 16384
NB = 256
F_DESC = 8
NBLK = 64
BR = 16
BC = 8
N_PROW = 4
N_PCOL = 8


KERNEL_SCALE = 8.0


RIDGE = 0.5


def draw_kernel(key, part):
    first_key = jax.random.fold_in(jax.random.fold_in(key, 7), 0)
    descriptors = jax.random.normal(first_key, (M, F_DESC), jnp.float32)
    column_numbers = jnp.arange(M, dtype=jnp.int32)

    def kernel_rows(start):
        segment = lax.dynamic_slice_in_dim(descriptors, start, NB, 0)
        distance = jnp.sum((segment[:, None, :] - descriptors[None, :, :]) ** 2, axis=2)
        diagonal = (start + jnp.arange(NB, dtype=jnp.int32))[:, None] == column_numbers[None, :]
        return jnp.exp(-distance / KERNEL_SCALE) + jnp.where(diagonal, RIDGE, 0.0)
    starts = jnp.arange(NBLK, dtype=jnp.int32) * NB
    values = lax.map(kernel_rows, starts)
    return values.reshape(BR, NBLK // BR, NB, BC, NBLK // BC, NB).astype(jnp.float32)


def draw_pivots(key, part):
    other_key, order_key = jax.random.split(jax.random.fold_in(key, 3))
    other = jax.random.randint(other_key, (), 0, NBLK - 1, dtype=jnp.int32)
    newest = jnp.full((), NBLK - 1, dtype=jnp.int32)
    flipped = jax.random.randint(order_key, (), 0, 2, dtype=jnp.int32) == 1
    first = jnp.where(flipped, other, newest)
    second = jnp.where(flipped, newest, other)
    return jnp.stack([first, second]).astype(jnp.int32)


def setup_inputs(seed: int = 0) -> dict:
    key_of = jax.random.split(jax.random.key(seed), 3)
    kernel = draw_kernel(jax.random.fold_in(key_of[2], 71), 0)
    pivots = draw_pivots(jax.random.fold_in(key_of[2], 71), 0)
    return {"kernel": kernel, "pivots": pivots}


HIGHEST = lax.Precision.HIGHEST

def pivot_step(matrix, pivot_block):
    start_row = (pivot_block * NB).astype(jnp.int32)
    column = lax.dynamic_slice_in_dim(matrix, start_row, NB, 1)
    diagonal = lax.dynamic_slice_in_dim(column, start_row, NB, 0)
    identity = jnp.eye(NB, dtype=jnp.float32)
    factor = jnp.linalg.cholesky(diagonal)
    inverse = lax.linalg.triangular_solve(factor, identity, left_side=True, lower=True)
    panel_rows = jnp.dot(column.astype(jnp.float32), inverse.T.astype(jnp.float32), precision=HIGHEST, preferred_element_type=jnp.float32)
    matrix = matrix - jnp.dot(panel_rows.astype(jnp.float32), panel_rows.T.astype(jnp.float32), precision=HIGHEST, preferred_element_type=jnp.float32)
    block_ids = (jnp.arange(M, dtype=jnp.int32) // NB).astype(jnp.int32)
    retained = block_ids != pivot_block.astype(jnp.int32)
    matrix = jnp.where(retained[:, None] & retained[None, :], matrix, jnp.zeros((), jnp.float32))
    return (panel_rows, matrix)

def reference(kernel, pivots):
    matrix = kernel.reshape(M, M)
    first_rows, matrix = pivot_step(matrix, pivots[0])
    second_rows, matrix = pivot_step(matrix, pivots[1])
    panels = jnp.stack([first_rows, second_rows]).reshape(2, BR, N_PROW, NB, NB)
    trailing = matrix.reshape(BR, N_PROW, NB, BC, N_PCOL, NB)
    return (panels, trailing)
```

```python
import functools

import jax
import jax.numpy as jnp
from jax import lax
from jax.experimental import pallas as pl
from jax.experimental.pallas import tpu as pltpu
from jax.sharding import PartitionSpec as P

HIGHEST = lax.Precision.HIGHEST
MESH = pl.DeviceIdType.MESH
F32 = jnp.float32
BF16 = jnp.bfloat16


def dot(a, b, dims=((1,), (0,))):
    return lax.dot_general(a, b, (dims, ((), ())), precision=HIGHEST, preferred_element_type=F32)


def spread_kernel(
    pivot_column, nrow, ncol, col_ref, row_ref, wrow_ref, wcol_ref,
    ring_recv, ring_send, pair_send, z_recv, up_send, down_send, local_sem,
):
    r = lax.axis_index("prow")
    c = lax.axis_index("pcol")
    chip, core = c // 2, c % 2
    chips = ncol // 2
    order = [p ^ (p >> 1) for p in range(chips)]
    place = {ch: p for p, ch in enumerate(order)}

    def lookup(values):
        total = 0
        for ch in range(chips):
            total = total + jnp.where(chip == ch, values[ch], 0)
        return total

    position = lookup([place[ch] for ch in range(chips)])
    nxt = lookup([order[(place[ch] + 1) % chips] for ch in range(chips)]) * 2 + core
    prv = lookup([order[(place[ch] - 1) % chips] for ch in range(chips)]) * 2 + core
    sibling = chip * 2 + 1 - core

    barrier = pltpu.get_barrier_semaphore()
    for other in (nxt, prv, sibling):
        pl.semaphore_signal(barrier, inc=1, device_id={"pcol": other}, device_id_type=MESH)

    @pl.when(r > 0)
    def _():
        pl.semaphore_signal(barrier, inc=1, device_id={"prow": r - 1}, device_id_type=MESH)

    @pl.when(r < nrow - 1)
    def _():
        pl.semaphore_signal(barrier, inc=1, device_id={"prow": r + 1}, device_id_type=MESH)

    peers = 3 + jnp.where(r > 0, 1, 0) + jnp.where(r < nrow - 1, 1, 0)
    pl.semaphore_wait(barrier, peers)

    row_blocks, col_blocks = wrow_ref.shape[1], wcol_ref.shape[1]
    half = row_blocks // 2
    root_columns = (ncol - 1, pivot_column)
    root_rows = ((ncol - 1) % nrow, pivot_column % nrow)

    def ring_state(s):
        root = root_columns[s]
        rel = (position - place[root // 2] + chips) % chips
        return rel, core == root % 2

    def ring_copy(s, b, src, target):
        return pltpu.make_async_remote_copy(
            src_ref=src.at[s, b], dst_ref=wrow_ref.at[s, b],
            send_sem=ring_send.at[s, b], recv_sem=ring_recv.at[s, b],
            device_id={"pcol": target}, device_id_type=MESH,
        )

    def pair_copy(s, b, src):
        return pltpu.make_async_remote_copy(
            src_ref=src.at[s, b], dst_ref=wrow_ref.at[s, b],
            send_sem=pair_send.at[s, b], recv_sem=ring_recv.at[s, b],
            device_id={"pcol": sibling}, device_id_type=MESH,
        )

    def z_copy(s, j, src, sems, target):
        return pltpu.make_async_remote_copy(
            src_ref=src.at[s, j], dst_ref=wcol_ref.at[s, j],
            send_sem=sems.at[s, j], recv_sem=z_recv.at[s, j],
            device_id={"prow": target}, device_id_type=MESH,
        )

    def local_row(s):
        return pltpu.make_async_copy(col_ref.at[s], wrow_ref.at[s], local_sem.at[s])

    def local_col(s):
        return pltpu.make_async_copy(row_ref.at[s], wcol_ref.at[s], local_sem.at[2 + s])

    def ring_step(s, b):
        rel, member = ring_state(s)
        forward = b < half
        target = nxt if forward else prv
        onward = (rel < chips - 1) if forward else (rel != 1)

        @pl.when(member & (rel == 0))
        def _():
            ring_copy(s, b, col_ref, target).start()
            pair_copy(s, b, col_ref).start()

        @pl.when(member & (rel != 0))
        def _():
            ring_copy(s, b, wrow_ref, target).wait_recv()

            @pl.when(onward)
            def _():
                ring_copy(s, b, wrow_ref, target).start()

            pair_copy(s, b, wrow_ref).start()

    def z_step(s, j):
        root = root_rows[s]

        @pl.when(r == root)
        def _():
            if root < nrow - 1:
                z_copy(s, j, row_ref, up_send, r + 1).start()
            if root > 0:
                z_copy(s, j, row_ref, down_send, r - 1).start()

        if root < nrow - 1:
            @pl.when(r > root)
            def _():
                z_copy(s, j, wcol_ref, up_send, r).wait_recv()

                @pl.when(r < nrow - 1)
                def _():
                    z_copy(s, j, wcol_ref, up_send, r + 1).start()

        if root > 0:
            @pl.when(r < root)
            def _():
                z_copy(s, j, wcol_ref, down_send, r).wait_recv()

                @pl.when(r > 0)
                def _():
                    z_copy(s, j, wcol_ref, down_send, r - 1).start()

    for step in range(max(half, col_blocks)):
        for s in range(2):
            if step < col_blocks:
                z_step(s, step)
        for s in range(2):
            if step < half:
                ring_step(s, step)
                ring_step(s, half + step)

    for s in range(2):
        rel, member = ring_state(s)

        @pl.when(member & (rel == 0))
        def _():
            local_row(s).start()

        @pl.when(r == root_rows[s])
        def _():
            local_col(s).start()

    for s in range(2):
        rel, member = ring_state(s)
        for b in range(row_blocks):
            forward = b < half
            onward = ((rel < chips - 1) if forward else (rel != 1)) | (rel == 0)

            @pl.when(member & onward)
            def _():
                ring_copy(s, b, wrow_ref, nxt).wait_send()

            @pl.when(member)
            def _():
                pair_copy(s, b, wrow_ref).wait_send()

            @pl.when(jnp.logical_not(member))
            def _():
                pair_copy(s, b, wrow_ref).wait_recv()

        root = root_rows[s]
        for j in range(col_blocks):
            if root < nrow - 1:
                @pl.when((r >= root) & (r < nrow - 1))
                def _():
                    z_copy(s, j, wcol_ref, up_send, r).wait_send()
            if root > 0:
                @pl.when((r <= root) & (r > 0))
                def _():
                    z_copy(s, j, wcol_ref, down_send, r).wait_send()

        @pl.when(member & (rel == 0))
        def _():
            local_row(s).wait()

        @pl.when(r == root)
        def _():
            local_col(s).wait()


def spread(pivot_column, nrow, ncol, columns, rows):
    anyspace = pl.BlockSpec(memory_space=pl.ANY)
    dma = pltpu.SemaphoreType.DMA
    br, bc = columns.shape[1], rows.shape[1]
    return pl.pallas_call(
        functools.partial(spread_kernel, pivot_column, nrow, ncol),
        out_shape=[
            jax.ShapeDtypeStruct(columns.shape, F32),
            jax.ShapeDtypeStruct(rows.shape, F32),
        ],
        in_specs=[anyspace] * 2,
        out_specs=[anyspace] * 2,
        scratch_shapes=[
            dma((2, br)), dma((2, br)), dma((2, br)),
            dma((2, bc)), dma((2, bc)), dma((2, bc)), dma((4,)),
        ],
        compiler_params=pltpu.CompilerParams(
            collective_id=pivot_column, has_side_effects=True
        ),
        name="spread",
    )(columns, rows)


SMALL = 64


def small_inverse(block):
    n = SMALL
    rows = lax.broadcasted_iota(jnp.int32, (n, n), 0)
    lanes = lax.broadcasted_iota(jnp.int32, (n, n), 1)
    table = jnp.concatenate([block, jnp.where(rows == lanes, 1.0, 0.0)], axis=1)
    below = lax.broadcasted_iota(jnp.int32, (n, 1), 0)
    diagonal = jnp.ones((n, 1), F32)
    for k in range(n):
        column = table[:, k : k + 1]
        row = table[k : k + 1, :]
        pivot = table[k : k + 1, k : k + 1]
        diagonal = jnp.where(below == k, pivot, diagonal)
        if k < n - 1:
            table = table - jnp.where(below > k, column, 0.0) * (row * (1.0 / pivot))
    return table[:, n:] * lax.rsqrt(diagonal)


def factor_into(work_ref, inverse_ref):
    n = work_ref.shape[0]
    for start in range(0, n, SMALL):
        stop = start + SMALL
        lead = small_inverse(work_ref[start:stop, start:stop])
        rows = dot(lead, work_ref[start:stop, :])
        inverse_ref[start:stop, :] = rows[:, n:]
        if stop < n:
            work_ref[stop:, :] = work_ref[stop:, :] - dot(
                rows[:, stop:n], rows, ((0,), (0,))
            )


def factor_kernel(d_ref, first_ref, cross_ref, second_ref, work_ref):
    n = d_ref.shape[1]
    eye = jnp.where(
        lax.broadcasted_iota(jnp.int32, (n, n), 0) == lax.broadcasted_iota(jnp.int32, (n, n), 1),
        1.0, 0.0,
    ).astype(F32)
    work_ref[:, :n] = d_ref[0]
    work_ref[:, n:] = eye
    factor_into(work_ref, first_ref)
    cross = dot(d_ref[1], first_ref[...], ((1,), (1,)))
    cross_ref[...] = cross
    work_ref[:, :n] = d_ref[2] - dot(cross, cross, ((1,), (1,)))
    work_ref[:, n:] = eye
    factor_into(work_ref, second_ref)


def factors(blocks):
    n = blocks.shape[1]
    square = jax.ShapeDtypeStruct((n, n), F32)
    return pl.pallas_call(
        factor_kernel,
        out_shape=[square, square, square],
        scratch_shapes=[pltpu.VMEM((n, 2 * n), F32)],
        compiler_params=pltpu.CompilerParams(vmem_limit_bytes=32 << 20),
        name="factors",
    )(blocks)


def split(x):
    high = x.astype(BF16)
    return high, (x - high.astype(F32)).astype(BF16)


def update_kernel(
    nrow, ncol, scal_ref, a_ref, w0_ref, w1_ref, g0_ref, g1_ref,
    first_ref, cross_ref, second_ref, panel_ref, out_ref, right_ref,
):
    i = pl.program_id(0)
    p0, p1, r, c = scal_ref[2], scal_ref[3], scal_ref[4], scal_ref[5]
    n = first_ref.shape[0]
    blocks = g0_ref.shape[1]
    first, cross, second = first_ref[...], cross_ref[...], second_ref[...]

    @pl.when(i == 0)
    def _():
        for j in range(blocks):
            f = dot(first, g0_ref[0, j])
            s = dot(second, g1_ref[0, j] - dot(cross, f))
            at = slice(j * n, (j + 1) * n)
            for t, x in enumerate((f, s)):
                high, low = split(x)
                right_ref[t * n : (t + 1) * n, at] = high
                right_ref[(2 + t) * n : (3 + t) * n, at] = low
                right_ref[(4 + t) * n : (5 + t) * n, at] = high

    block_row = i * nrow + r
    f = dot(w0_ref[0, 0], first, ((1,), (1,)))
    rest = w1_ref[0, 0] - dot(f, cross, ((1,), (1,)))
    rest = jnp.where(block_row == p0, 0.0, rest)
    s = dot(rest, second, ((1,), (1,)))
    panel_ref[0, 0] = f
    panel_ref[1, 0] = s
    f_high, f_low = split(f)
    s_high, s_low = split(s)
    left = jnp.concatenate([f_high, s_high, f_high, s_high, f_low, s_low], axis=1)
    row_kept = (block_row != p0) & (block_row != p1)
    stride = 2 * blocks
    for j in range(blocks):
        block_column = j * ncol + c
        kept = row_kept & (block_column != p0) & (block_column != p1)
        product = lax.dot_general(
            left, right_ref[:, j * n : (j + 1) * n], (((1,), (0,)), ((), ())),
            preferred_element_type=F32,
        )
        for h in range(2):
            rows = pl.ds(2 * j + h, n, stride=stride)
            value = a_ref[rows, :] - product[:, h * 128 : (h + 1) * 128]
            out_ref[rows, :] = jnp.where(kept, value, 0.0)


def update(nrow, ncol, scal, flat, wrow, wcol, first, cross, second):
    _, br, n, _ = wrow.shape
    bc = wcol.shape[1]
    per_row = n * bc * n // 128
    whole = pl.BlockSpec((n, n), lambda i, sc: (0, 0))
    return pl.pallas_call(
        functools.partial(update_kernel, nrow, ncol),
        grid_spec=pltpu.PrefetchScalarGridSpec(
            num_scalar_prefetch=1,
            grid=(br,),
            in_specs=[
                pl.BlockSpec((per_row, 128), lambda i, sc: (i, 0)),
                pl.BlockSpec((1, 1, n, n), lambda i, sc: (sc[0], i, 0, 0)),
                pl.BlockSpec((1, 1, n, n), lambda i, sc: (sc[1], i, 0, 0)),
                pl.BlockSpec((1, bc, n, n), lambda i, sc: (sc[0], 0, 0, 0)),
                pl.BlockSpec((1, bc, n, n), lambda i, sc: (sc[1], 0, 0, 0)),
                whole, whole, whole,
            ],
            out_specs=[
                pl.BlockSpec((2, 1, n, n), lambda i, sc: (0, i, 0, 0)),
                pl.BlockSpec((per_row, 128), lambda i, sc: (i, 0)),
            ],
            scratch_shapes=[pltpu.VMEM((6 * n, bc * n), BF16)],
        ),
        out_shape=[
            jax.ShapeDtypeStruct((2, br, n, n), F32),
            jax.ShapeDtypeStruct(flat.shape, F32),
        ],
        compiler_params=pltpu.CompilerParams(vmem_limit_bytes=56 << 20),
        name="update",
    )(scal, flat, wrow, wrow, wcol, wcol, first, cross, second)


def shards(kernel, pivots):
    br, _, n, bc, _, _ = kernel.shape
    nrow, ncol = lax.axis_size("prow"), lax.axis_size("pcol")
    r, c = lax.axis_index("prow"), lax.axis_index("pcol")
    matrix = kernel.reshape(br, n, bc, n)
    newest = br * nrow - 1
    p0, p1 = pivots[0], pivots[1]
    flipped = p0 != newest
    other = jnp.where(flipped, p0, p1)

    def entry(row, column):
        block = lax.dynamic_slice(
            matrix, (row // nrow, 0, column // ncol, 0), (1, n, 1, n)
        ).reshape(n, n)
        here = (row % nrow == r) & (column % ncol == c)
        return jnp.where(here, block, 0.0)

    corner = lax.psum(
        jnp.stack([entry(p0, p0), entry(p1, p0), entry(p1, p1)]), ("prow", "pcol")
    )
    columns = jnp.stack([
        matrix[:, :, bc - 1, :],
        lax.dynamic_index_in_dim(matrix, other // ncol, 2, keepdims=False),
    ])
    rows = jnp.stack([
        matrix[br - 1],
        lax.dynamic_index_in_dim(matrix, other // nrow, 0, keepdims=False),
    ]).transpose(0, 2, 1, 3)
    wrow, wcol = lax.switch(
        other % ncol,
        [functools.partial(spread, k, nrow, ncol) for k in range(ncol)],
        columns, rows,
    )
    first, cross, second = factors(corner)
    slot = flipped.astype(jnp.int32)
    scal = jnp.stack([slot, 1 - slot, p0, p1, r, c]).astype(jnp.int32)
    flat = kernel.reshape(-1, 128)
    panels, trailing = update(nrow, ncol, scal, flat, wrow, wcol, first, cross, second)
    return panels.reshape(2, br, 1, n, n), trailing.reshape(kernel.shape)


def solution(mesh):
    in_specs = (P(None, "prow", None, None, "pcol", None), P())
    out_specs = (P(None, None, "prow", None, None), P(None, "prow", None, None, "pcol", None))
    return jax.shard_map(shards, mesh=mesh, in_specs=in_specs, out_specs=out_specs, check_vma=False)
```

```python
import functools

import jax
import jax.numpy as jnp
from jax import lax
from jax.experimental import pallas as pl
from jax.experimental.pallas import tpu as pltpu
from jax.sharding import PartitionSpec as P

HIGHEST = lax.Precision.HIGHEST
F32 = jnp.float32
BF16 = jnp.bfloat16


def dot(a, b, dims=((1,), (0,))):
    return lax.dot_general(a, b, (dims, ((), ())), precision=HIGHEST, preferred_element_type=F32)


SMALL = 64


def small_inverse(block):
    n = SMALL
    rows = lax.broadcasted_iota(jnp.int32, (n, n), 0)
    lanes = lax.broadcasted_iota(jnp.int32, (n, n), 1)
    table = jnp.concatenate([block, jnp.where(rows == lanes, 1.0, 0.0)], axis=1)
    below = lax.broadcasted_iota(jnp.int32, (n, 1), 0)
    diagonal = jnp.ones((n, 1), F32)
    for k in range(n):
        column = table[:, k : k + 1]
        row = table[k : k + 1, :]
        pivot = table[k : k + 1, k : k + 1]
        diagonal = jnp.where(below == k, pivot, diagonal)
        if k < n - 1:
            table = table - jnp.where(below > k, column, 0.0) * (row * (1.0 / pivot))
    return table[:, n:] * lax.rsqrt(diagonal)


def factor_into(work_ref, inverse_ref):
    n = work_ref.shape[0]
    for start in range(0, n, SMALL):
        stop = start + SMALL
        lead = small_inverse(work_ref[start:stop, start:stop])
        rows = dot(lead, work_ref[start:stop, :])
        inverse_ref[start:stop, :] = rows[:, n:]
        if stop < n:
            work_ref[stop:, :] = work_ref[stop:, :] - dot(
                rows[:, stop:n], rows, ((0,), (0,))
            )


def factor_kernel(d_ref, first_ref, cross_ref, second_ref, work_ref):
    n = d_ref.shape[1]
    eye = jnp.where(
        lax.broadcasted_iota(jnp.int32, (n, n), 0) == lax.broadcasted_iota(jnp.int32, (n, n), 1),
        1.0, 0.0,
    ).astype(F32)
    work_ref[:, :n] = d_ref[0]
    work_ref[:, n:] = eye
    factor_into(work_ref, first_ref)
    cross = dot(d_ref[1], first_ref[...], ((1,), (1,)))
    cross_ref[...] = cross
    work_ref[:, :n] = d_ref[2] - dot(cross, cross, ((1,), (1,)))
    work_ref[:, n:] = eye
    factor_into(work_ref, second_ref)


def factors(blocks):
    n = blocks.shape[1]
    square = jax.ShapeDtypeStruct((n, n), F32)
    return pl.pallas_call(
        factor_kernel,
        out_shape=[square, square, square],
        scratch_shapes=[pltpu.VMEM((n, 2 * n), F32)],
        compiler_params=pltpu.CompilerParams(vmem_limit_bytes=32 << 20),
        name="factors",
    )(blocks)


def split(x):
    high = x.astype(BF16)
    return high, (x - high.astype(F32)).astype(BF16)


def update_kernel(
    nrow, ncol, scal_ref, a_ref, w0_ref, w1_ref, g0_ref, g1_ref,
    first_ref, cross_ref, second_ref, panel_ref, out_ref, right_ref,
):
    i = pl.program_id(0)
    p0, p1, r, c = scal_ref[2], scal_ref[3], scal_ref[4], scal_ref[5]
    n = first_ref.shape[0]
    blocks = g0_ref.shape[1]
    first, cross, second = first_ref[...], cross_ref[...], second_ref[...]

    @pl.when(i == 0)
    def _():
        for j in range(blocks):
            f = dot(first, g0_ref[0, j])
            s = dot(second, g1_ref[0, j] - dot(cross, f))
            at = slice(j * n, (j + 1) * n)
            for t, x in enumerate((f, s)):
                high, low = split(x)
                right_ref[t * n : (t + 1) * n, at] = high
                right_ref[(2 + t) * n : (3 + t) * n, at] = low
                right_ref[(4 + t) * n : (5 + t) * n, at] = high

    block_row = i * nrow + r
    f = dot(w0_ref[0, 0], first, ((1,), (1,)))
    rest = w1_ref[0, 0] - dot(f, cross, ((1,), (1,)))
    rest = jnp.where(block_row == p0, 0.0, rest)
    s = dot(rest, second, ((1,), (1,)))
    panel_ref[0, 0] = f
    panel_ref[1, 0] = s
    f_high, f_low = split(f)
    s_high, s_low = split(s)
    left = jnp.concatenate([f_high, s_high, f_high, s_high, f_low, s_low], axis=1)
    row_kept = (block_row != p0) & (block_row != p1)
    stride = 2 * blocks
    for j in range(blocks):
        block_column = j * ncol + c
        kept = row_kept & (block_column != p0) & (block_column != p1)
        product = lax.dot_general(
            left, right_ref[:, j * n : (j + 1) * n], (((1,), (0,)), ((), ())),
            preferred_element_type=F32,
        )
        for h in range(2):
            rows = pl.ds(2 * j + h, n, stride=stride)
            value = a_ref[rows, :] - product[:, h * 128 : (h + 1) * 128]
            out_ref[rows, :] = jnp.where(kept, value, 0.0)


def update(nrow, ncol, scal, flat, wrow, wcol, first, cross, second):
    _, br, n, _ = wrow.shape
    bc = wcol.shape[1]
    per_row = n * bc * n // 128
    whole = pl.BlockSpec((n, n), lambda i, sc: (0, 0))
    return pl.pallas_call(
        functools.partial(update_kernel, nrow, ncol),
        grid_spec=pltpu.PrefetchScalarGridSpec(
            num_scalar_prefetch=1,
            grid=(br,),
            in_specs=[
                pl.BlockSpec((per_row, 128), lambda i, sc: (i, 0)),
                pl.BlockSpec((1, 1, n, n), lambda i, sc: (sc[0], i, 0, 0)),
                pl.BlockSpec((1, 1, n, n), lambda i, sc: (sc[1], i, 0, 0)),
                pl.BlockSpec((1, bc, n, n), lambda i, sc: (sc[0], 0, 0, 0)),
                pl.BlockSpec((1, bc, n, n), lambda i, sc: (sc[1], 0, 0, 0)),
                whole, whole, whole,
            ],
            out_specs=[
                pl.BlockSpec((2, 1, n, n), lambda i, sc: (0, i, 0, 0)),
                pl.BlockSpec((per_row, 128), lambda i, sc: (i, 0)),
            ],
            scratch_shapes=[pltpu.VMEM((6 * n, bc * n), BF16)],
        ),
        out_shape=[
            jax.ShapeDtypeStruct((2, br, n, n), F32),
            jax.ShapeDtypeStruct(flat.shape, F32),
        ],
        compiler_params=pltpu.CompilerParams(vmem_limit_bytes=56 << 20),
        name="update",
    )(scal, flat, wrow, wrow, wcol, wcol, first, cross, second)


def shards(kernel, pivots):
    br, _, n, bc, _, _ = kernel.shape
    nrow, ncol = lax.axis_size("prow"), lax.axis_size("pcol")
    r, c = lax.axis_index("prow"), lax.axis_index("pcol")
    matrix = kernel.reshape(br, n, bc, n)
    p0, p1 = pivots[0], pivots[1]

    def entry(row, column):
        slab = lax.dynamic_index_in_dim(matrix, row // nrow, 0, keepdims=False)
        block = lax.dynamic_index_in_dim(slab, column // ncol, 1, keepdims=False)
        here = (row % nrow == r) & (column % ncol == c)
        return jnp.where(here, block, 0.0)

    corner = lax.psum(
        jnp.stack([entry(p0, p0), entry(p1, p0), entry(p1, p1)]), ("prow", "pcol")
    )
    first, cross, second = factors(corner)
    columns = jnp.stack([
        jnp.where(
            c == p % ncol,
            lax.dynamic_index_in_dim(matrix, p // ncol, 2, keepdims=False),
            0.0,
        )
        for p in (p0, p1)
    ])
    wrow = lax.psum(columns, "pcol")
    rows = jnp.stack([
        jnp.where(
            r == p % nrow,
            lax.dynamic_index_in_dim(matrix, p // nrow, 0, keepdims=False),
            0.0,
        )
        for p in (p0, p1)
    ]).transpose(0, 2, 1, 3)
    wcol = lax.psum(rows, "prow")
    scal = jnp.stack([0 * p0, 0 * p0 + 1, p0, p1, r, c]).astype(jnp.int32)
    flat = kernel.reshape(-1, 128)
    panels, trailing = update(nrow, ncol, scal, flat, wrow, wcol, first, cross, second)
    return panels.reshape(2, br, 1, n, n), trailing.reshape(kernel.shape)


def solution(mesh):
    in_specs = (P(None, "prow", None, None, "pcol", None), P())
    out_specs = (P(None, None, "prow", None, None), P(None, "prow", None, None, "pcol", None))
    return jax.shard_map(shards, mesh=mesh, in_specs=in_specs, out_specs=out_specs, check_vma=False)
```
